256 devices in a mesh: section: 4 (over x), hidden: 8 (over y, core), tok: 8 (over z).
Axes of the slice: x: 4, y: 4, z: 8, core: 2. Of those that a mesh axis runs over, the one named last changes fastest.
Arguments:
- section_inputs: bfloat16 [4, 3072, 16384], P('section', 'tok', 'hidden'), may hold values from -6 to 6
- top_adjoint: bfloat16 [3072, 16384], P('tok', 'hidden'), may hold values from -6 to 6
- right_first: bfloat16 [4, 128, 128, 128], P('section', ('hidden', 'tok')), may hold values from -0.5 to 0.5
- left_first: bfloat16 [4, 128, 128, 128], P('section', ('hidden', 'tok')), may hold values from -0.5 to 0.5
- right_second: bfloat16 [4, 128, 128, 128], P('section', ('hidden', 'tok')), may hold values from -0.5 to 0.5
- left_second: bfloat16 [4, 128, 128, 128], P('section', ('hidden', 'tok')), may hold values from -0.5 to 0.5
Outputs:
- input_adjoint: bfloat16 [4, 3072, 16384], P('section', 'tok', 'hidden')
- grad_right_first: float32 [4, 128, 128, 128], P('section', ('hidden', 'tok'))
- grad_left_first: float32 [4, 128, 128, 128], P('section', ('hidden', 'tok'))
- grad_right_second: float32 [4, 128, 128, 128], P('section', ('hidden', 'tok'))
- grad_left_second: float32 [4, 128, 128, 128], P('section', ('hidden', 'tok'))
The draws below stay inside these ranges and needn't reach their ends.
All inputs are finite; a program needn't handle non-finite values.
Results may differ from the reference program's by a relative error of at most 0.02.
Values may be sent and summed in bfloat16 or wider, within the bound.
A program may use at most 64 MiB of HBM per device.

```python
import math
import jax
import jax.numpy as jnp

BLK = 128
D = 16384
TOKENS = 3072
N_SECTION = 4


def block_scale(key, dims, cuts, smallest, high):
    def one(position, parts):
        heights = jax.random.uniform(jax.random.fold_in(jax.random.fold_in(key, 6), position), (parts,), jnp.float32, smallest / len(cuts), high / len(cuts))
        return jnp.repeat(jnp.exp(heights), dims[position] // parts).reshape((-1,) + (1,) * (len(dims) - position - 1))

    gain = one(*cuts[0])
    for cut in cuts[1:]:
        gain = gain * one(*cut)
    return gain


def scatter_about(key, shape, spread, bound, shards=(), dtype=jnp.bfloat16):
    values = spread * jax.random.normal(key, shape, jnp.float32)
    if shards:
        values = values * block_scale(key, shape, shards, -0.22, 0.18)
    return jnp.clip(values, -bound, bound).astype(dtype)


def setup_inputs(seed: int = 0) -> dict:
    splits = jax.random.split(jax.random.key(seed), 7)
    return {
        "section_inputs": scatter_about(splits[0], (N_SECTION, TOKENS, D), 1.0, 6.0, ((0, 4), (1, 8), (2, 8))),
        "top_adjoint": scatter_about(splits[1], (TOKENS, D), 1.0, 6.0, ((0, 8), (1, 8))),
        "right_first": scatter_about(splits[2], (N_SECTION, BLK, BLK, BLK), BLK ** -0.5, 0.5, ((0, 4), (1, 64))),
        "left_first": scatter_about(splits[3], (N_SECTION, BLK, BLK, BLK), BLK ** -0.5, 0.5, ((0, 4), (1, 64))),
        "right_second": scatter_about(splits[4], (N_SECTION, BLK, BLK, BLK), BLK ** -0.5, 0.5, ((0, 4), (1, 64))),
        "left_second": scatter_about(splits[5], (N_SECTION, BLK, BLK, BLK), BLK ** -0.5, 0.5, ((0, 4), (1, 64))),
    }


gelu_coef = 0.7978845608028654

def gelu_parts(preact):
    inner_arg = gelu_coef * (preact + 0.044715 * preact * preact * preact)
    squashed = jnp.tanh(inner_arg)
    activation = 0.5 * preact * (1.0 + squashed)
    derivative = 0.5 * (1.0 + squashed) + 0.5 * preact * (1.0 - squashed * squashed) * gelu_coef * (1.0 + 3.0 * 0.044715 * preact * preact)
    return (activation, derivative)

def as_float(array):
    return array.astype(jnp.float32)

def reference(section_inputs, top_adjoint, right_first, left_first, right_second, left_second):
    grad_scale = 1.0 / math.sqrt(TOKENS)
    upstream = top_adjoint.reshape(TOKENS, BLK, BLK)
    adjoint_list = []
    list_right_first = []
    list_left_first = []
    list_right_second = []
    list_left_second = []
    for section_id in range(N_SECTION - 1, -1, -1):
        inputs = section_inputs[section_id].reshape(TOKENS, BLK, BLK)
        weight_rf = as_float(right_first[section_id])
        weight_lf = as_float(left_first[section_id])
        weight_rs = as_float(right_second[section_id])
        weight_ls = as_float(left_second[section_id])
        first_mid = jnp.einsum('tbi,bji->tbj', as_float(inputs), weight_rf).astype(jnp.bfloat16)
        first_out = jnp.einsum('tbj,jkb->tjk', as_float(first_mid), weight_lf)
        activation, derivative = gelu_parts(first_out)
        activation = activation.astype(jnp.bfloat16)
        second_mid = jnp.einsum('tbi,bji->tbj', as_float(activation), weight_rs).astype(jnp.bfloat16)
        upstream_f = as_float(upstream)
        grad_ls = grad_scale * jnp.einsum('tjk,tbj->jkb', upstream_f, as_float(second_mid))
        grad_mid_second = jnp.einsum('tjk,jkb->tbj', upstream_f, weight_ls).astype(jnp.bfloat16)
        grad_rs = grad_scale * jnp.einsum('tbj,tbi->bji', as_float(grad_mid_second), as_float(activation))
        grad_activation = jnp.einsum('tbj,bji->tbi', as_float(grad_mid_second), weight_rs)
        grad_pre = (grad_activation * derivative).astype(jnp.bfloat16)
        grad_lf = grad_scale * jnp.einsum('tjk,tbj->jkb', as_float(grad_pre), as_float(first_mid))
        grad_mid_first = jnp.einsum('tjk,jkb->tbj', as_float(grad_pre), weight_lf).astype(jnp.bfloat16)
        grad_rf = grad_scale * jnp.einsum('tbj,tbi->bji', as_float(grad_mid_first), as_float(inputs))
        grad_input = jnp.einsum('tbj,bji->tbi', as_float(grad_mid_first), weight_rf)
        adjoint = (upstream_f + grad_input).astype(jnp.bfloat16)
        adjoint_list.append(adjoint.reshape(TOKENS, D))
        list_right_first.append(grad_rf)
        list_left_first.append(grad_lf)
        list_right_second.append(grad_rs)
        list_left_second.append(grad_ls)
        upstream = adjoint
    input_adjoint = jnp.stack(adjoint_list[::-1], axis=0)
    return (input_adjoint, jnp.stack(list_right_first[::-1], axis=0), jnp.stack(list_left_first[::-1], axis=0), jnp.stack(list_right_second[::-1], axis=0), jnp.stack(list_left_second[::-1], axis=0))
```

```python
import math

import jax
import jax.numpy as jnp
from jax import lax
from jax.sharding import PartitionSpec as P

MICRO = 3
gelu_coef = 0.7978845608028654


def passed_along(block, axis, distance):
    devices = range(lax.axis_size(axis))
    route = [(i - distance, i) for i in devices if i - distance in devices]
    return lax.ppermute(block, axis, route)


def gelu_parts(preact):
    inner_arg = gelu_coef * (preact + 0.044715 * preact * preact * preact)
    squashed = jnp.tanh(inner_arg)
    activation = 0.5 * preact * (1.0 + squashed)
    derivative = 0.5 * (1.0 + squashed) + 0.5 * preact * (1.0 - squashed * squashed) * gelu_coef * (
        1.0 + 3.0 * 0.044715 * preact * preact
    )
    return (activation, derivative)


def swap_blocks(values):
    return lax.all_to_all(values, "hidden", split_axis=0, concat_axis=1, tiled=True)


def dot(spec, a, b):
    return jnp.einsum(spec, a, b, preferred_element_type=jnp.float32)


def on_device(section_inputs, top_adjoint, right_first, left_first, right_second, left_second):
    bf = jnp.bfloat16
    sections = lax.axis_size("section")
    section_id = lax.axis_index("section")
    rf, lf, rs, ls = (
        lax.all_gather(w[0], "tok", axis=0, tiled=True)
        for w in (right_first, left_first, right_second, left_second)
    )
    local, size = rf.shape[0], rf.shape[1]
    tokens, width = top_adjoint.shape
    rows = tokens // MICRO
    scale = 1.0 / math.sqrt(tokens * lax.axis_size("tok"))
    x = section_inputs[0].reshape(tokens, local, size)
    first_mid = swap_blocks(dot("tbi,bji->jbt", x, rf).astype(bf))
    first_out = dot("jbt,jkb->jkt", first_mid, lf)
    act, der = gelu_parts(first_out)
    act = act.astype(bf)
    second_mid = swap_blocks(dot("bit,bji->jbt", act, rs).astype(bf))

    def run_tick(tick, state):
        incoming, ups_all, gm2_all, gpre_all, gm1_all, out_all = state
        micro = tick - (sections - 1 - section_id)
        active = jnp.logical_and(micro >= 0, micro < MICRO)
        start = jnp.clip(micro, 0, MICRO - 1) * rows
        top_rows = lax.dynamic_slice_in_dim(top_adjoint, start, rows, 0)
        ups_flat = jnp.where(section_id == sections - 1, top_rows, incoming)
        ups = ups_flat.reshape(rows, local, size)
        gm2 = swap_blocks(dot("tjk,jkb->bjt", ups, ls).astype(bf))
        gact = dot("bjt,bji->bit", gm2, rs)
        gpre = (gact * lax.dynamic_slice_in_dim(der, start, rows, 2)).astype(bf)
        gm1 = swap_blocks(dot("jkt,jkb->bjt", gpre, lf).astype(bf))
        ginp = dot("bjt,bji->tbi", gm1, rf)
        adjoint = (ups.astype(jnp.float32) + ginp).astype(bf).reshape(rows, width)

        def keep(whole, part, axis):
            old = lax.dynamic_slice_in_dim(whole, start, rows, axis)
            return lax.dynamic_update_slice_in_dim(whole, jnp.where(active, part, old), start, axis)

        return (
            passed_along(adjoint, "section", -1),
            keep(ups_all, ups_flat, 0),
            keep(gm2_all, gm2, 2),
            keep(gpre_all, gpre, 2),
            keep(gm1_all, gm1, 2),
            keep(out_all, adjoint, 0),
        )

    wide = jnp.zeros((local, size, tokens), bf)
    flat = jnp.zeros((tokens, width), bf)
    state = (jnp.zeros((rows, width), bf), flat, wide, wide, wide, flat)
    _, ups_all, gm2, gpre, gm1, adjoints = lax.fori_loop(0, MICRO + sections - 1, run_tick, state)
    ups = ups_all.reshape(tokens, local, size)
    g_ls = dot("tjk,jbt->jkb", ups, second_mid)
    g_rs = dot("bjt,bit->bji", gm2, act)
    g_lf = dot("jkt,jbt->jkb", gpre, first_mid)
    g_rf = dot("bjt,tbi->bji", gm1, x)
    g_rf, g_lf, g_rs, g_ls = (
        scale
        * lax.psum_scatter(g.astype(bf), "tok", scatter_dimension=0, tiled=True).astype(jnp.float32)
        for g in (g_rf, g_lf, g_rs, g_ls)
    )
    return adjoints[None], g_rf[None], g_lf[None], g_rs[None], g_ls[None]


def solution(mesh):
    act = P("section", "tok", "hidden")
    weight = P("section", ("hidden", "tok"), None, None)
    return jax.shard_map(
        on_device,
        mesh=mesh,
        in_specs=(act, P("tok", "hidden"), weight, weight, weight, weight),
        out_specs=(act, weight, weight, weight, weight),
        check_vma=False,
    )
```

```python
import functools
import math

import jax
import jax.numpy as jnp
from jax import lax
from jax.experimental import pallas as pl
from jax.experimental.pallas import tpu as pltpu
from jax.sharding import PartitionSpec as P

MESH = pl.DeviceIdType.MESH
BF, F32 = jnp.bfloat16, jnp.float32
BLK = 128
MIC = 128
GRP = 4
COEF = 0.7978845608028654
FM, SM, GM2, GM1 = range(4)
RF, LF, RS, LS = range(4)


def gelu_parts(v):
    squashed = jnp.tanh(COEF * (v + 0.044715 * v * v * v))
    activation = 0.5 * v * (1.0 + squashed)
    derivative = 0.5 * (1.0 + squashed) + 0.5 * v * (1.0 - squashed * squashed) * COEF * (
        1.0 + 3.0 * 0.044715 * v * v
    )
    return activation, derivative


def nn(a, b):
    return lax.dot_general(a, b, (((1,), (0,)), ((), ())), preferred_element_type=F32)


def nt(a, b):
    return lax.dot_general(a, b, (((1,), (1,)), ((), ())), preferred_element_type=F32)


def tn(a, b):
    return lax.dot_general(a, b, (((0,), (0,)), ((), ())), preferred_element_type=F32)


def lanes(b, count=1):
    return pl.ds(pl.multiple_of(b * BLK, BLK), count * BLK)


def kernel(
    S, H, Z, scale,
    x, top, rf, lf, rs, ls,
    adj, o_rf, o_lf, o_rs, o_ls,
    ups, send, recv, act, der, gpre, stage, weights, turned, sums, part_send, part_recv,
    top_sem, w_send, w_recv, a_send, a_recv, p_send, p_recv, r_send, r_recv,
):
    sec, h, z = (lax.axis_index(name) for name in ("section", "hidden", "tok"))
    is_last, is_first = sec == S - 1, sec == 0
    below, above = lax.rem(sec + S - 1, S), lax.rem(sec + 1, S)
    M = x.shape[0] // MIC
    NB = x.shape[1] // BLK
    SH = NB // Z
    groups = NB // GRP

    def rows(m):
        return pl.ds(m * MIC, MIC)

    def wait(view, sem):
        pltpu.make_async_copy(view, view, sem).wait()

    top_copy = pltpu.make_async_copy(top, ups, top_sem)

    @pl.when(is_last)
    def _():
        top_copy.start()

    barrier = pltpu.get_barrier_semaphore()
    for off in range(1, H):
        pl.semaphore_signal(barrier, 1, device_id={"hidden": lax.rem(h + off, H)}, device_id_type=MESH)
    for off in range(1, Z):
        pl.semaphore_signal(barrier, 1, device_id={"tok": lax.rem(z + off, Z)}, device_id_type=MESH)

    for peer in (below, above):
        pl.semaphore_signal(barrier, 1, device_id={"section": peer}, device_id_type=MESH)

    mine = pl.ds(z * SH, SH)
    for s in range(SH):
        weights[LS, z * SH + s] = ls[s].astype(F32).T.astype(BF)
    weights[RF, mine] = rf[...]
    weights[LF, mine] = lf[...]
    weights[RS, mine] = rs[...]

    pl.semaphore_wait(barrier, H - 1 + Z - 1 + 2)

    for f in (RF, LF, LS, RS):
        for off in range(1, Z):
            pltpu.make_async_remote_copy(
                src_ref=weights.at[f, mine],
                dst_ref=weights.at[f, mine],
                send_sem=w_send.at[f],
                recv_sem=w_recv.at[f],
                device_id={"tok": lax.rem(z + off, Z)},
                device_id_type=MESH,
            ).start()

    for f in range(4):
        sums[f] = jnp.zeros_like(sums[f])

    def wait_weights(f):
        wait(weights.at[f, pl.ds(0, (Z - 1) * SH)], w_recv.at[f])

    def over_groups(body, before=None, after=None):
        def group(g, carry):
            if before is not None:
                before(g)
            for u in range(GRP):
                body(g * GRP + u)
            if after is not None:
                after(g)
            return carry

        lax.fori_loop(0, groups, group, 0)

    def put(block, value):
        stage[pl.ds(block, BLK, stride=NB), :] = value

    def staged(d):
        part = pl.ds(pl.multiple_of(d * NB * NB, NB * NB), NB * NB)
        return stage[part, :].astype(BF).reshape(NB, NB, MIC)

    def exchange(p, m):
        slot = pl.ds(pl.multiple_of(h * NB, NB), NB)
        for off in sorted(range(1, H), key=lambda o: abs(o - H // 2)):
            peer = lax.rem(h + off, H)
            send[p, m, peer] = staged(peer)
            pltpu.make_async_remote_copy(
                src_ref=send.at[p, m, peer],
                dst_ref=recv.at[p, m, :, slot, :],
                send_sem=a_send.at[p, m],
                recv_sem=a_recv.at[p, m],
                device_id={"hidden": peer},
                device_id_type=MESH,
            ).start()
        recv[p, m, :, slot, :] = staged(h)

    def wait_exchange(p, m):
        wait(recv.at[p, m, pl.ds(0, NB - NB // H)], a_recv.at[p, m])

    def first_mid(m):
        over_groups(lambda b: put(b, nt(weights[RF, b], x[rows(m), lanes(b)])))
        exchange(FM, m)

    def activations(m):
        def body(j):
            a, d = gelu_parts(nn(weights[LF, j], recv[FM, m, j]))
            act[m, j] = a.astype(BF)
            der[m, j] = d

        wait_exchange(FM, m)
        over_groups(body)

    def second_mid(m):
        over_groups(lambda b: put(b, nn(weights[RS, b], act[m, b])))
        exchange(SM, m)

    def grad_mid_second(m, arrives):
        def before(g):
            wait(ups.at[rows(m), lanes(g * GRP, GRP)], p_recv.at[m, g])

        over_groups(
            lambda j: put(j, nt(weights[LS, j], ups[rows(m), lanes(j)])),
            before=before if arrives else None,
        )
        exchange(GM2, m)

    def grad_mid_first(m):
        def body(b):
            pre = (nn(turned[1, b], recv[GM2, m, b]) * der[m, b]).astype(BF)
            gpre[m, b] = pre
            put(b, nn(turned[0, b], pre))

        wait_exchange(GM2, m)
        over_groups(body)
        exchange(GM1, m)

    def input_adjoint(m):
        def body(b):
            at = lanes(b)
            grad = tn(recv[GM1, m, b], weights[RF, b])
            adj[rows(m), at] = (ups[rows(m), at].astype(F32) + grad).astype(BF)

        def after(g):
            @pl.when(jnp.logical_not(is_first))
            def _():
                part = lanes(g * GRP, GRP)
                pltpu.make_async_remote_copy(
                    src_ref=adj.at[rows(m), part],
                    dst_ref=ups.at[rows(m), part],
                    send_sem=p_send.at[m, g],
                    recv_sem=p_recv.at[m, g],
                    device_id={"section": below},
                    device_id_type=MESH,
                ).start()

        wait_exchange(GM1, m)
        over_groups(body, after=after)

    def wide_gradients(m):
        def body(b):
            sums[RS, b] += nt(recv[GM2, m, b], act[m, b])
            sums[LF, b] += nt(gpre[m, b], recv[FM, m, b])

        over_groups(body)

    def gradient_rf(m):
        def body(b):
            sums[RF, b] += nn(recv[GM1, m, b], x[rows(m), lanes(b)])

        over_groups(body)

    def gradient_ls(m):
        def body(j):
            sums[LS, j] += nn(recv[SM, m, j], ups[rows(m), lanes(j)])

        wait_exchange(SM, m)
        over_groups(body)

    def scatter(f):
        for off in range(1, Z):
            peer = lax.rem(z + off, Z)
            theirs = pl.ds(peer * SH, SH)
            part_send[f, theirs] = sums[f, theirs].astype(BF)
            pltpu.make_async_remote_copy(
                src_ref=part_send.at[f, theirs],
                dst_ref=part_recv.at[f, z],
                send_sem=r_send.at[f],
                recv_sem=r_recv.at[f],
                device_id={"tok": peer},
                device_id_type=MESH,
            ).start()

    def collect(f, out, turn=False):
        wait(part_recv.at[f, pl.ds(0, Z - 1)], r_recv.at[f])
        for s in range(SH):
            total = sums[f, z * SH + s]
            for off in range(1, Z):
                total = total + part_recv[f, lax.rem(z + off, Z), s].astype(F32)
            total = scale * total
            out[s] = total.T if turn else total

    wait_weights(RF)
    for m in range(M):
        first_mid(m)
    wait_weights(LF)
    wait_weights(LS)

    @pl.when(is_last)
    def _():
        top_copy.wait()
        for m in range(M):
            grad_mid_second(m, False)

    wait_weights(RS)

    def turn(b):
        turned[0, b] = weights[LF, b].astype(F32).T.astype(BF)
        turned[1, b] = weights[RS, b].astype(F32).T.astype(BF)

    over_groups(turn)
    for m in range(M):
        activations(m)

        @pl.when(jnp.logical_not(is_last))
        def _():
            second_mid(m)

    def begin(m):
        @pl.when(jnp.logical_not(is_last))
        def _():
            grad_mid_second(m, True)
            gradient_ls(m)

    begin(0)
    for m in range(M):
        grad_mid_first(m)
        wide_gradients(m)
        if m + 1 < M:
            begin(m + 1)
        else:
            scatter(RS)
            scatter(LF)
        input_adjoint(m)
        gradient_rf(m)
    scatter(RF)

    @pl.when(is_last)
    def _():
        for m in range(M):
            second_mid(m)
        for m in range(M):
            gradient_ls(m)

    scatter(LS)
    collect(RS, o_rs)
    collect(LF, o_lf)
    collect(RF, o_rf)
    collect(LS, o_ls, True)

    for f in range(4):
        wait(weights.at[f, pl.ds(0, (Z - 1) * SH)], w_send.at[f])
        wait(part_send.at[f, pl.ds(0, (Z - 1) * SH)], r_send.at[f])
    for p in range(4):
        for m in range(M):
            wait(send.at[p, m, pl.ds(0, H - 1)], a_send.at[p, m])

    @pl.when(jnp.logical_not(is_first))
    def _():
        for m in range(M):
            for g in range(groups):
                wait(adj.at[rows(m), lanes(g * GRP, GRP)], p_send.at[m, g])


def solution(mesh):
    S, H, Z = (mesh.shape[name] for name in ("section", "hidden", "tok"))

    def on_device(section_inputs, top_adjoint, right_first, left_first, right_second, left_second):
        tokens, width = top_adjoint.shape
        M, NB, SH = tokens // MIC, width // BLK, right_first.shape[1]
        groups = NB // GRP
        scale = 1.0 / math.sqrt(tokens * Z)
        vmem = pl.BlockSpec(memory_space=pltpu.VMEM)
        dma = pltpu.SemaphoreType.DMA
        shard = jax.ShapeDtypeStruct((SH, BLK, BLK), F32)
        outs = pl.pallas_call(
            functools.partial(kernel, S, H, Z, scale),
            out_shape=[jax.ShapeDtypeStruct((tokens, width), BF)] + [shard] * 4,
            in_specs=[vmem, pl.BlockSpec(memory_space=pl.ANY)] + [vmem] * 4,
            out_specs=[vmem] * 5,
            scratch_shapes=[
                pltpu.VMEM((tokens, width), BF),
                pltpu.VMEM((4, M, H, NB, NB, MIC), BF),
                pltpu.VMEM((4, M, NB, BLK, MIC), BF),
                pltpu.VMEM((M, NB, BLK, MIC), BF),
                pltpu.VMEM((M, NB, BLK, MIC), F32),
                pltpu.VMEM((M, NB, BLK, MIC), BF),
                pltpu.VMEM((NB * BLK, MIC), F32),
                pltpu.VMEM((4, NB, BLK, BLK), BF),
                pltpu.VMEM((2, NB, BLK, BLK), BF),
                pltpu.VMEM((4, NB, BLK, BLK), F32),
                pltpu.VMEM((4, NB, BLK, BLK), BF),
                pltpu.VMEM((4, Z, SH, BLK, BLK), BF),
                dma,
                dma((4,)),
                dma((4,)),
                dma((4, M)),
                dma((4, M)),
                dma((M, groups)),
                dma((M, groups)),
                dma((4,)),
                dma((4,)),
            ],
            compiler_params=pltpu.CompilerParams(
                collective_id=0, has_side_effects=True, vmem_limit_bytes=56 * 1024 * 1024
            ),
        )(section_inputs[0], top_adjoint, right_first[0], left_first[0], right_second[0], left_second[0])
        return tuple(o[None] for o in outs)

    act = P("section", "tok", "hidden")
    weight = P("section", ("hidden", "tok"), None, None)
    return jax.shard_map(
        on_device,
        mesh=mesh,
        in_specs=(act, P("tok", "hidden"), weight, weight, weight, weight),
        out_specs=(act, weight, weight, weight, weight),
        check_vma=False,
    )
```

```python
import functools
import math

import jax
import jax.numpy as jnp
from jax import lax
from jax.experimental import pallas as pl
from jax.experimental.pallas import tpu as pltpu
from jax.sharding import PartitionSpec as P

MESH = pl.DeviceIdType.MESH
BF, F32 = jnp.bfloat16, jnp.float32
BLK = 128
MIC = 128
GRP = 4
COEF = 0.7978845608028654
FM, SM, GM2, GM1 = range(4)
RF, LF, RS, LS = range(4)


def gelu_parts(v):
    squashed = jnp.tanh(COEF * (v + 0.044715 * v * v * v))
    activation = 0.5 * v * (1.0 + squashed)
    derivative = 0.5 * (1.0 + squashed) + 0.5 * v * (1.0 - squashed * squashed) * COEF * (
        1.0 + 3.0 * 0.044715 * v * v
    )
    return activation, derivative


def nn(a, b):
    return lax.dot_general(a, b, (((1,), (0,)), ((), ())), preferred_element_type=F32)


def nt(a, b):
    return lax.dot_general(a, b, (((1,), (1,)), ((), ())), preferred_element_type=F32)


def tn(a, b):
    return lax.dot_general(a, b, (((0,), (0,)), ((), ())), preferred_element_type=F32)


def lanes(b, count=1):
    return pl.ds(pl.multiple_of(b * BLK, BLK), count * BLK)


def kernel(
    S, H, Z, scale,
    x, top, rf, lf, rs, ls,
    adj, o_rf, o_lf, o_rs, o_ls,
    ups, send, recv, act, der, gpre, stage, weights, turned, sums, part_send, part_recv,
    top_sem, w_send, w_recv, a_send, a_recv, p_send, p_recv, r_send, r_recv,
):
    sec, h, z = (lax.axis_index(name) for name in ("section", "hidden", "tok"))
    is_last, is_first = sec == S - 1, sec == 0
    below, above = lax.rem(sec + S - 1, S), lax.rem(sec + 1, S)
    M = x.shape[0] // MIC
    NB = x.shape[1] // BLK
    SH = NB // Z
    groups = NB // GRP

    def rows(m):
        return pl.ds(m * MIC, MIC)

    def wait(view, sem):
        pltpu.make_async_copy(view, view, sem).wait()

    top_copy = pltpu.make_async_copy(top, ups, top_sem)

    @pl.when(is_last)
    def _():
        top_copy.start()

    barrier = pltpu.get_barrier_semaphore()
    for off in range(1, H):
        pl.semaphore_signal(barrier, 1, device_id={"hidden": lax.rem(h + off, H)}, device_id_type=MESH)
    for off in range(1, Z):
        pl.semaphore_signal(barrier, 1, device_id={"tok": lax.rem(z + off, Z)}, device_id_type=MESH)

    for peer in (below, above):
        pl.semaphore_signal(barrier, 1, device_id={"section": peer}, device_id_type=MESH)

    mine = pl.ds(z * SH, SH)
    for s in range(SH):
        weights[LS, z * SH + s] = ls[s].astype(F32).T.astype(BF)
    weights[RF, mine] = rf[...]
    weights[LF, mine] = lf[...]
    weights[RS, mine] = rs[...]

    for f in range(4):
        sums[f] = jnp.zeros_like(sums[f])

    pl.semaphore_wait(barrier, H - 1 + Z - 1 + 2)

    def hops(f, way):
        return Z // 2 if way == f % 2 else Z - 1 - Z // 2

    def next_on(way):
        return {"tok": lax.rem(z + (1 if way == 0 else Z - 1), Z)}

    def ahead(way, distance):
        return lax.rem(z + (distance if way == 0 else Z - distance), Z)

    def share(index):
        return pl.ds(index * SH, SH)

    def gather_step(f, k):
        for way in (0, 1):
            if k < hops(f, way):
                part = weights.at[f, share(ahead(1 - way, k) if k else z)]
                if k:
                    wait(part, w_recv.at[f, way, k - 1])
                pltpu.make_async_remote_copy(
                    src_ref=part,
                    dst_ref=part,
                    send_sem=w_send.at[f],
                    recv_sem=w_recv.at[f, way, k],
                    device_id=next_on(way),
                    device_id_type=MESH,
                ).start()

    def gather_end(f):
        for way in (0, 1):
            wait(weights.at[f, share(0)], w_recv.at[f, way, hops(f, way) - 1])

    def scatter_step(f, k):
        for way in (0, 1):
            n = hops(f, way)
            if k < n:
                target = ahead(way, n - k)
                if k:
                    wait(part_recv.at[f, way, k - 1], r_recv.at[f, way, k - 1])
                for s in range(SH):
                    total = sums[f, target * SH + s]
                    if k:
                        total = total + part_recv[f, way, k - 1, s].astype(F32)
                    part_send[f, way, k, s] = total.astype(BF)
                pltpu.make_async_remote_copy(
                    src_ref=part_send.at[f, way, k],
                    dst_ref=part_recv.at[f, way, k],
                    send_sem=r_send.at[f],
                    recv_sem=r_recv.at[f, way, k],
                    device_id=next_on(way),
                    device_id_type=MESH,
                ).start()

    def collect(f, out, turn=False):
        for way in (0, 1):
            last = hops(f, way) - 1
            wait(part_recv.at[f, way, last], r_recv.at[f, way, last])
        for s in range(SH):
            total = sums[f, z * SH + s]
            for way in (0, 1):
                total = total + part_recv[f, way, hops(f, way) - 1, s].astype(F32)
            total = scale * total
            out[s] = total.T if turn else total

    def over_groups(body, before=None, after=None):
        def group(g, carry):
            if before is not None:
                before(g)
            for u in range(GRP):
                body(g * GRP + u)
            if after is not None:
                after(g)
            return carry

        lax.fori_loop(0, groups, group, 0)

    def put(block, value):
        stage[pl.ds(block, BLK, stride=NB), :] = value

    slot = pl.ds(pl.multiple_of(h * NB, NB), NB)

    def staged(d, g):
        at = pl.multiple_of((d * NB + g * GRP) * NB, NB)
        return stage[pl.ds(at, GRP * NB), :].astype(BF).reshape(GRP, NB, MIC)

    def exchange(p, m):
        def quarter(g, carry):
            part = pl.ds(g * GRP, GRP)
            for off in sorted(range(1, H), key=lambda o: abs(o - H // 2)):
                peer = lax.rem(h + off, H)
                send[p, m, peer, part] = staged(peer, g)
                pltpu.make_async_remote_copy(
                    src_ref=send.at[p, m, peer, part],
                    dst_ref=recv.at[p, m, part, slot, :],
                    send_sem=a_send.at[p, m],
                    recv_sem=a_recv.at[p, m, g],
                    device_id={"hidden": peer},
                    device_id_type=MESH,
                ).start()
            recv[p, m, part, slot, :] = staged(h, g)
            return carry

        lax.fori_loop(0, groups, quarter, 0)

    def arrival(p, m):
        def before(g):
            wait(recv.at[p, m, pl.ds(g * GRP, GRP), pl.ds(0, BLK - NB)], a_recv.at[p, m, g])

        return before

    def first_mid(m):
        over_groups(lambda b: put(b, nt(weights[RF, b], x[rows(m), lanes(b)])))
        exchange(FM, m)

    def activations(m):
        def body(j):
            a, d = gelu_parts(nn(weights[LF, j], recv[FM, m, j]))
            act[m, j] = a.astype(BF)
            der[m, j] = d

        over_groups(body, before=arrival(FM, m))

    def second_mid(m):
        over_groups(lambda b: put(b, nn(weights[RS, b], act[m, b])))
        exchange(SM, m)

    def grad_mid_second(m, arrives):
        def before(g):
            wait(ups.at[rows(m), lanes(g * GRP, GRP)], p_recv.at[m, g])

        over_groups(
            lambda j: put(j, nt(weights[LS, j], ups[rows(m), lanes(j)])),
            before=before if arrives else None,
        )
        exchange(GM2, m)

    def grad_mid_first(m):
        def body(b):
            pre = (nn(turned[1, b], recv[GM2, m, b]) * der[m, b]).astype(BF)
            gpre[m, b] = pre
            put(b, nn(turned[0, b], pre))

        over_groups(body, before=arrival(GM2, m))
        exchange(GM1, m)

    def input_adjoint(m):
        def body(b):
            at = lanes(b)
            grad = tn(recv[GM1, m, b], weights[RF, b])
            adj[rows(m), at] = (ups[rows(m), at].astype(F32) + grad).astype(BF)

        def after(g):
            @pl.when(jnp.logical_not(is_first))
            def _():
                part = lanes(g * GRP, GRP)
                pltpu.make_async_remote_copy(
                    src_ref=adj.at[rows(m), part],
                    dst_ref=ups.at[rows(m), part],
                    send_sem=p_send.at[m, g],
                    recv_sem=p_recv.at[m, g],
                    device_id={"section": below},
                    device_id_type=MESH,
                ).start()

        over_groups(body, before=arrival(GM1, m), after=after)

    def wide_gradients(m):
        def body(b):
            sums[RS, b] += nt(recv[GM2, m, b], act[m, b])
            sums[LF, b] += nt(gpre[m, b], recv[FM, m, b])

        over_groups(body)

    def gradient_rf(m):
        def body(b):
            sums[RF, b] += nn(recv[GM1, m, b], x[rows(m), lanes(b)])

        over_groups(body)

    def gradient_ls(m):
        def body(j):
            sums[LS, j] += nn(recv[SM, m, j], ups[rows(m), lanes(j)])

        over_groups(body, before=arrival(SM, m))

    def turn(b):
        turned[0, b] = weights[LF, b].astype(F32).T.astype(BF)
        turned[1, b] = weights[RS, b].astype(F32).T.astype(BF)

    steps = Z // 2
    for k in range(steps):
        gather_step(RF, k)
        gather_step(LS, k)
    gather_step(LF, 0)
    gather_step(RS, 0)
    gather_end(RF)
    gather_end(LS)

    def more(k):
        for f in (LF, RS):
            if k < steps:
                gather_step(f, k)
            else:
                gather_end(f)

    def chain_of_last():
        top_copy.wait()
        first_mid(0)
        grad_mid_second(0, False)
        more(1)
        first_mid(1)
        grad_mid_second(1, False)
        more(2)
        more(3)
        more(4)
        over_groups(turn)
        activations(0)
        grad_mid_first(0)
        first_mid(2)
        grad_mid_second(2, False)
        activations(1)
        grad_mid_first(1)
        input_adjoint(0)
        activations(2)
        grad_mid_first(2)
        input_adjoint(1)
        wide_gradients(0)
        input_adjoint(2)
        for m in range(M):
            second_mid(m)
        gradient_rf(0)
        for m in range(1, M):
            wide_gradients(m)
            gradient_rf(m)
        for m in range(M):
            gradient_ls(m)
        for f in (RS, LF, LS):
            scatter_step(f, 0)
        for f in (RS, LF, LS):
            scatter_step(f, 1)

    def chain_of_others():
        for m in range(M):
            first_mid(m)
            more(m + 1)
        gather_end(LF)
        activations(0)
        gather_end(RS)
        second_mid(0)
        for m in range(1, M):
            activations(m)
            second_mid(m)
        over_groups(turn)

        def begin(m):
            grad_mid_second(m, True)
            gradient_ls(m)

        begin(0)
        for m in range(M):
            grad_mid_first(m)
            if m + 1 == M:
                scatter_step(LS, 0)
            wide_gradients(m)
            if m + 1 < M:
                begin(m + 1)
            else:
                scatter_step(RS, 0)
                scatter_step(LF, 0)
                scatter_step(LS, 1)
            input_adjoint(m)
            if m + 1 == M:
                scatter_step(RS, 1)
                scatter_step(LF, 1)
            gradient_rf(m)

    pl.when(is_last)(chain_of_last)
    pl.when(jnp.logical_not(is_last))(chain_of_others)

    scatter_step(RF, 0)
    scatter_step(LS, 2)
    scatter_step(RS, 2)
    scatter_step(LF, 2)
    scatter_step(RF, 1)
    scatter_step(LS, 3)
    scatter_step(RS, 3)
    scatter_step(LF, 3)
    scatter_step(RF, 2)
    collect(LS, o_ls, True)
    scatter_step(RF, 3)
    collect(RS, o_rs)
    collect(LF, o_lf)
    collect(RF, o_rf)

    for f in range(4):
        wait(weights.at[f, pl.ds(0, (Z - 1) * SH)], w_send.at[f])
        wait(weights.at[f, pl.ds(0, (Z - 1) * SH)], r_send.at[f])
    for p in range(4):
        for m in range(M):
            wait(send.at[p, m, pl.ds(0, H - 1)], a_send.at[p, m])

    @pl.when(jnp.logical_not(is_first))
    def _():
        for m in range(M):
            for g in range(groups):
                wait(adj.at[rows(m), lanes(g * GRP, GRP)], p_send.at[m, g])


def solution(mesh):
    S, H, Z = (mesh.shape[name] for name in ("section", "hidden", "tok"))

    def on_device(section_inputs, top_adjoint, right_first, left_first, right_second, left_second):
        tokens, width = top_adjoint.shape
        M, NB, SH = tokens // MIC, width // BLK, right_first.shape[1]
        groups = NB // GRP
        scale = 1.0 / math.sqrt(tokens * Z)
        vmem = pl.BlockSpec(memory_space=pltpu.VMEM)
        dma = pltpu.SemaphoreType.DMA
        shard = jax.ShapeDtypeStruct((SH, BLK, BLK), F32)
        outs = pl.pallas_call(
            functools.partial(kernel, S, H, Z, scale),
            out_shape=[jax.ShapeDtypeStruct((tokens, width), BF)] + [shard] * 4,
            in_specs=[vmem, pl.BlockSpec(memory_space=pl.ANY)] + [vmem] * 4,
            out_specs=[vmem] * 5,
            scratch_shapes=[
                pltpu.VMEM((tokens, width), BF),
                pltpu.VMEM((4, M, H, NB, NB, MIC), BF),
                pltpu.VMEM((4, M, NB, BLK, MIC), BF),
                pltpu.VMEM((M, NB, BLK, MIC), BF),
                pltpu.VMEM((M, NB, BLK, MIC), F32),
                pltpu.VMEM((M, NB, BLK, MIC), BF),
                pltpu.VMEM((NB * BLK, MIC), F32),
                pltpu.VMEM((4, NB, BLK, BLK), BF),
                pltpu.VMEM((2, NB, BLK, BLK), BF),
                pltpu.VMEM((4, NB, BLK, BLK), F32),
                pltpu.VMEM((4, 2, Z // 2, SH, BLK, BLK), BF),
                pltpu.VMEM((4, 2, Z // 2, SH, BLK, BLK), BF),
                dma,
                dma((4,)),
                dma((4, 2, Z // 2)),
                dma((4, M)),
                dma((4, M, groups)),
                dma((M, groups)),
                dma((M, groups)),
                dma((4,)),
                dma((4, 2, Z // 2)),
            ],
            compiler_params=pltpu.CompilerParams(
                collective_id=0, has_side_effects=True, vmem_limit_bytes=56 * 1024 * 1024
            ),
        )(section_inputs[0], top_adjoint, right_first[0], left_first[0], right_second[0], left_second[0])
        return tuple(o[None] for o in outs)

    act = P("section", "tok", "hidden")
    weight = P("section", ("hidden", "tok"), None, None)
    return jax.shard_map(
        on_device,
        mesh=mesh,
        in_specs=(act, P("tok", "hidden"), weight, weight, weight, weight),
        out_specs=(act, weight, weight, weight, weight),
        check_vma=False,
    )
```

```python
import functools
import math

import jax
import jax.numpy as jnp
from jax import lax
from jax.experimental import pallas as pl
from jax.experimental.pallas import tpu as pltpu
from jax.sharding import PartitionSpec as P

MESH = pl.DeviceIdType.MESH
BF, F32 = jnp.bfloat16, jnp.float32
BLK = 128
MIC = 64
LANES = 2 * MIC
GRP = 4
COEF = 0.7978845608028654
FM, SM, GM2, GM1 = range(4)
RF, LF, RS, LS = range(4)


def gelu_parts(v):
    squashed = jnp.tanh(COEF * (v + 0.044715 * v * v * v))
    activation = 0.5 * v * (1.0 + squashed)
    derivative = 0.5 * (1.0 + squashed) + 0.5 * v * (1.0 - squashed * squashed) * COEF * (
        1.0 + 3.0 * 0.044715 * v * v
    )
    return activation, derivative


def nn(a, b):
    return lax.dot_general(a, b, (((1,), (0,)), ((), ())), preferred_element_type=F32)


def nt(a, b):
    return lax.dot_general(a, b, (((1,), (1,)), ((), ())), preferred_element_type=F32)


def tn(a, b):
    return lax.dot_general(a, b, (((0,), (0,)), ((), ())), preferred_element_type=F32)


def lanes(b, count=1):
    return pl.ds(pl.multiple_of(b * BLK, BLK), count * BLK)


def kernel(
    S, H, Z, scale,
    x, top, rf, lf, rs, ls,
    adj, grads,
    ups, send, recv, act, der, gpre, stage, weights, turned, sums, part_send, part_recv,
    top_sem, w_send, w_recv, a_send, a_recv, p_send, p_recv, r_send, r_recv,
):
    sec, h, z = (lax.axis_index(name) for name in ("section", "hidden", "tok"))
    is_last, is_first = sec == S - 1, sec == 0
    early = sec < S - 2
    below, above = lax.rem(sec + S - 1, S), lax.rem(sec + 1, S)
    M = x.shape[0] // MIC
    NB = x.shape[1] // BLK
    SH = NB // Z
    half = NB // 2
    groups = half // GRP

    def rows(m):
        return pl.ds(pl.multiple_of(m * MIC, MIC), MIC)

    def wait(view, sem):
        pltpu.make_async_copy(view, view, sem).wait()

    top_copy = pltpu.make_async_copy(top, ups, top_sem)

    @pl.when(is_last)
    def _():
        top_copy.start()

    barrier = pltpu.get_barrier_semaphore()
    for off in range(1, H):
        pl.semaphore_signal(barrier, 1, device_id={"hidden": lax.rem(h + off, H)}, device_id_type=MESH)
    for off in range(1, Z):
        pl.semaphore_signal(barrier, 1, device_id={"tok": lax.rem(z + off, Z)}, device_id_type=MESH)

    for peer in (below, above):
        pl.semaphore_signal(barrier, 1, device_id={"section": peer}, device_id_type=MESH)

    mine = pl.ds(z * SH, SH)
    for s in range(SH):
        weights[LS, z * SH + s] = ls[s].astype(F32).T.astype(BF)
    weights[RF, mine] = rf[...]
    weights[LF, mine] = lf[...]
    weights[RS, mine] = rs[...]

    for f in range(4):
        sums[f] = jnp.zeros_like(sums[f])

    pl.semaphore_wait(barrier, H - 1 + Z - 1 + 2)

    def hops(f, way):
        return Z // 2 if way == f % 2 else Z - 1 - Z // 2

    def next_on(way):
        return {"tok": lax.rem(z + (1 if way == 0 else Z - 1), Z)}

    def ahead(way, distance):
        return lax.rem(z + (distance if way == 0 else Z - distance), Z)

    def share(index):
        return pl.ds(index * SH, SH)

    def gather_step(f, k):
        for way in (0, 1):
            if k < hops(f, way):
                part = weights.at[f, share(ahead(1 - way, k) if k else z)]
                if k:
                    wait(part, w_recv.at[f, way, k - 1])
                pltpu.make_async_remote_copy(
                    src_ref=part,
                    dst_ref=part,
                    send_sem=w_send.at[f],
                    recv_sem=w_recv.at[f, way, k],
                    device_id=next_on(way),
                    device_id_type=MESH,
                ).start()

    def gather_end(f):
        for way in (0, 1):
            wait(weights.at[f, share(0)], w_recv.at[f, way, hops(f, way) - 1])

    def scatter_step(f, k):
        for way in (0, 1):
            n = hops(f, way)
            if k < n:
                target = ahead(way, n - k)
                if k:
                    wait(part_recv.at[f, way, k - 1], r_recv.at[f, way, k - 1])
                for s in range(SH):
                    total = sums[f, target * SH + s]
                    if k:
                        total = total + part_recv[f, way, k - 1, s].astype(F32)
                    part_send[f, way, k, s] = total.astype(BF)
                pltpu.make_async_remote_copy(
                    src_ref=part_send.at[f, way, k],
                    dst_ref=part_recv.at[f, way, k],
                    send_sem=r_send.at[f],
                    recv_sem=r_recv.at[f, way, k],
                    device_id=next_on(way),
                    device_id_type=MESH,
                ).start()

    def collect(f, turn=False):
        for way in (0, 1):
            last = hops(f, way) - 1
            wait(part_recv.at[f, way, last], r_recv.at[f, way, last])
        for s in range(SH):
            total = sums[f, z * SH + s]
            for way in (0, 1):
                total = total + part_recv[f, way, hops(f, way) - 1, s].astype(F32)
            total = scale * total
            grads[f, s] = total.T if turn else total

    def over_groups(body, before=None, after=None):
        def group(g, carry):
            if before is not None:
                before(g)
            for u in range(GRP):
                body(g * GRP + u)
            if after is not None:
                after(g)
            return carry

        lax.fori_loop(0, groups, group, 0)

    def low(*lead):
        shape = lead + (LANES,)
        return lax.broadcasted_iota(jnp.int32, shape, len(lead)) < MIC

    def put(block, value):
        stage[pl.ds(block, H * half, stride=NB), :] = value.reshape(H * half, LANES)

    def split(value):
        return value.reshape(H, 2, half, LANES)

    def twice(ref, m, b):
        value = ref[rows(m), lanes(b)]
        return jnp.concatenate([value, value], 0)

    def both(f, p):
        return jnp.concatenate([f[p], f[p + half]], 0)

    def diagonal(ref, m, p):
        zero = jnp.zeros((MIC, BLK), BF)
        upper = jnp.concatenate([ref[rows(m), lanes(p)], zero], 1)
        lower = jnp.concatenate([zero, ref[rows(m), lanes(p + half)]], 1)
        return jnp.concatenate([upper, lower], 0)

    def masked(value):
        zero = jnp.zeros_like(value)
        first = low(BLK)
        return jnp.concatenate([jnp.where(first, value, zero), jnp.where(first, zero, value)], 0)

    def put_narrow(weight, ref, m, p):
        for b in (p, p + half):
            out = split(nt(weight[b], twice(ref, m, b)))
            put(b, jnp.where(low(H, half), out[:, 0], out[:, 1]))

    def mine_of(value):
        return jnp.where(low(BLK), value[:BLK], value[BLK:])

    def put_wide(value, p):
        first, second, mask = split(value[:BLK]), split(value[BLK:]), low(H, half)
        other = jnp.where(mask, first[:, 1], second[:, 0]).reshape(H * half, LANES)
        other = pltpu.roll(other, MIC, 1).reshape(H, half, LANES)
        put(p, jnp.where(mask, first[:, 0], other))
        put(p + half, jnp.where(mask, other, second[:, 1]))

    slot = pl.ds(pl.multiple_of(h * NB, NB), NB)

    def staged(d, g):
        at = pl.multiple_of((d * half + g * GRP) * NB, NB)
        return stage[pl.ds(at, GRP * NB), :].astype(BF).reshape(GRP, NB, LANES)

    def exchange(p, m):
        def quarter(g, carry):
            part = pl.ds(g * GRP, GRP)
            for off in sorted(range(1, H), key=lambda o: abs(o - H // 2)):
                peer = lax.rem(h + off, H)
                send[p, m, peer, part] = staged(peer, g)
                pltpu.make_async_remote_copy(
                    src_ref=send.at[p, m, peer, part],
                    dst_ref=recv.at[p, m, part, slot, :],
                    send_sem=a_send.at[p, m],
                    recv_sem=a_recv.at[p, m, g],
                    device_id={"hidden": peer},
                    device_id_type=MESH,
                ).start()
            recv[p, m, part, slot, :] = staged(h, g)
            return carry

        lax.fori_loop(0, groups, quarter, 0)

    def arrival(p, m):
        def before(g):
            wait(recv.at[p, m, pl.ds(g * GRP, GRP), pl.ds(0, BLK - NB)], a_recv.at[p, m, g])

        return before

    def first_mid(m):
        over_groups(lambda p: put_narrow(weights.at[RF], x, m, p))
        exchange(FM, m)

    def activations(m):
        def body(p):
            a, d = gelu_parts(mine_of(nn(both(weights.at[LF], p), recv[FM, m, p])))
            act[m, p] = a.astype(BF)
            der[m, p] = d

        over_groups(body, before=arrival(FM, m))

    def second_mid(m):
        over_groups(lambda p: put_wide(nn(both(weights.at[RS], p), act[m, p]), p))
        exchange(SM, m)

    def passed(m, g, q):
        return rows(m), lanes(q * half + g * GRP, GRP)

    def grad_mid_second(m, arrives):
        def before(g):
            for q in (0, 1):
                wait(ups.at[passed(m, g, q)], p_recv.at[m, g, q])

        over_groups(
            lambda p: put_narrow(weights.at[LS], ups, m, p),
            before=before if arrives else None,
        )
        exchange(GM2, m)

    def grad_mid_first(m):
        def body(p):
            grad = mine_of(nn(both(turned.at[1], p), recv[GM2, m, p]))
            pre = (grad * der[m, p]).astype(BF)
            gpre[m, p] = pre
            put_wide(nn(both(turned.at[0], p), pre), p)

        over_groups(body, before=arrival(GM2, m))
        exchange(GM1, m)

    def input_adjoint(m):
        def body(p):
            weight = jnp.concatenate([weights[RF, p], weights[RF, p + half]], 1)
            grad = tn(recv[GM1, m, p], weight)
            for q in (0, 1):
                at = lanes(p + q * half)
                part = grad[q * MIC : (q + 1) * MIC, q * BLK : (q + 1) * BLK]
                adj[rows(m), at] = (ups[rows(m), at].astype(F32) + part).astype(BF)

        def after(g):
            @pl.when(jnp.logical_not(is_first))
            def _():
                for q in (0, 1):
                    part = passed(m, g, q)
                    pltpu.make_async_remote_copy(
                        src_ref=adj.at[part],
                        dst_ref=ups.at[part],
                        send_sem=p_send.at[m, g, q],
                        recv_sem=p_recv.at[m, g, q],
                        device_id={"section": below},
                        device_id_type=MESH,
                    ).start()

        over_groups(body, before=arrival(GM1, m), after=after)

    def wide_gradients(m):
        def body(p):
            for f, left, right in (
                (RS, recv[GM2, m, p], act[m, p]),
                (LF, gpre[m, p], recv[FM, m, p]),
            ):
                grad = nt(masked(left), right)
                sums[f, p] += grad[:BLK]
                sums[f, p + half] += grad[BLK:]

        over_groups(body)

    def narrow_gradient(f, m, p, left, ref):
        grad = nn(left, diagonal(ref, m, p))
        sums[f, p] += grad[:, :BLK]
        sums[f, p + half] += grad[:, BLK:]

    def gradient_rf(m):
        over_groups(lambda p: narrow_gradient(RF, m, p, recv[GM1, m, p], x))

    def gradient_ls(m):
        over_groups(
            lambda p: narrow_gradient(LS, m, p, recv[SM, m, p], ups), before=arrival(SM, m)
        )

    def turn(p):
        for b in (p, p + half):
            turned[0, b] = weights[LF, b].astype(F32).T.astype(BF)
            turned[1, b] = weights[RS, b].astype(F32).T.astype(BF)

    steps = Z // 2

    def advance(*items):
        for f, k in items:
            if k < steps:
                gather_step(f, k)
            else:
                gather_end(f)

    for k in range(steps):
        advance((RF, k), (LS, k))
    advance((LF, 0), (RS, 0), (RF, steps), (LS, steps))

    def repeat(first, end, body):
        def step(m, carry):
            body(m)
            return carry

        lax.fori_loop(first, end, step, 0)

    def chain_of_last():
        def feed(m):
            first_mid(m)
            grad_mid_second(m, False)

        def pull(m):
            activations(m)
            grad_mid_first(m)

        top_copy.wait()
        feed(0)
        advance((LF, 1), (RS, 1))
        feed(1)
        advance((LF, 2), (RS, 2), (LF, 3), (RS, 3), (LF, 4), (RS, 4))
        over_groups(turn)
        def steady(m):
            pull(m)
            feed(m + 2)
            input_adjoint(m)

        def ending(m):
            pull(m)
            input_adjoint(m)

        repeat(0, M - 2, steady)
        repeat(M - 2, M, ending)
        repeat(0, M, second_mid)

        def own_gradients(m):
            wide_gradients(m)
            gradient_rf(m)

        repeat(0, M, own_gradients)
        repeat(0, M, gradient_ls)
        for f, k in ((LS, 0), (RS, 0), (LF, 0), (LS, 1), (LS, 2), (LS, 3)):
            scatter_step(f, k)

    def chain_of_others():
        for k in range(1, steps):
            first_mid(k - 1)
            advance((LF, k), (RS, k))
        repeat(steps - 1, M, first_mid)
        advance((LF, steps), (RS, steps))

        def forward(m):
            activations(m)
            pl.when(early)(lambda: second_mid(m))

        repeat(0, M, forward)
        over_groups(turn)

        def steady(m):
            grad_mid_first(m)
            grad_mid_second(m + 1, True)
            wide_gradients(m)
            pl.when(early)(lambda: gradient_ls(m + 1))
            input_adjoint(m)
            gradient_rf(m)

        grad_mid_second(0, True)
        pl.when(early)(lambda: gradient_ls(0))
        repeat(0, M - 2, steady)
        m = M - 2
        grad_mid_first(m)
        grad_mid_second(m + 1, True)
        pl.when(early)(lambda: gradient_ls(M - 1))
        pl.when(early)(lambda: scatter_step(LS, 0))
        wide_gradients(m)
        input_adjoint(m)
        pl.when(early)(lambda: scatter_step(LS, 1))
        gradient_rf(m)
        m = M - 1
        grad_mid_first(m)
        pl.when(early)(lambda: scatter_step(LS, 2))
        wide_gradients(m)
        scatter_step(RS, 0)
        scatter_step(LF, 0)
        pl.when(early)(lambda: scatter_step(LS, 3))
        input_adjoint(m)
        gradient_rf(m)

        @pl.when(jnp.logical_not(early))
        def _():
            repeat(0, M, second_mid)
            repeat(0, M, gradient_ls)
            for k in range(steps):
                scatter_step(LS, k)

    pl.when(is_last)(chain_of_last)
    pl.when(jnp.logical_not(is_last))(chain_of_others)

    scatter_step(RF, 0)
    for k in range(1, steps):
        for f in (RS, LF, RF):
            scatter_step(f, k)
    collect(LS, True)
    collect(RS)
    collect(LF)
    collect(RF)

    for f in range(4):
        wait(weights.at[f, pl.ds(0, (Z - 1) * SH)], w_send.at[f])
        wait(weights.at[f, pl.ds(0, (Z - 1) * SH)], r_send.at[f])
    for p in range(4):
        for m in range(M):
            wait(send.at[p, m, pl.ds(0, H - 1)], a_send.at[p, m])

    @pl.when(jnp.logical_not(is_first))
    def _():
        for m in range(M):
            for g in range(groups):
                for q in (0, 1):
                    wait(adj.at[passed(m, g, q)], p_send.at[m, g, q])


def solution(mesh):
    S, H, Z = (mesh.shape[name] for name in ("section", "hidden", "tok"))

    def on_device(section_inputs, top_adjoint, right_first, left_first, right_second, left_second):
        tokens, width = top_adjoint.shape
        M, NB, SH = tokens // MIC, width // BLK, right_first.shape[1]
        half = NB // 2
        groups = half // GRP
        scale = 1.0 / math.sqrt(tokens * Z)
        vmem = pl.BlockSpec(memory_space=pltpu.VMEM)
        dma = pltpu.SemaphoreType.DMA
        adjoint, grads = pl.pallas_call(
            functools.partial(kernel, S, H, Z, scale),
            out_shape=[
                jax.ShapeDtypeStruct((tokens, width), BF),
                jax.ShapeDtypeStruct((4, SH, BLK, BLK), F32),
            ],
            in_specs=[vmem, pl.BlockSpec(memory_space=pl.ANY)] + [vmem] * 4,
            out_specs=[vmem] * 2,
            scratch_shapes=[
                pltpu.VMEM((tokens, width), BF),
                pltpu.VMEM((4, M, H, half, NB, LANES), BF),
                pltpu.VMEM((4, M, half, BLK, LANES), BF),
                pltpu.VMEM((M, half, BLK, LANES), BF),
                pltpu.VMEM((M, half, BLK, LANES), F32),
                pltpu.VMEM((M, half, BLK, LANES), BF),
                pltpu.VMEM((H * half * NB, LANES), F32),
                pltpu.VMEM((4, NB, BLK, BLK), BF),
                pltpu.VMEM((2, NB, BLK, BLK), BF),
                pltpu.VMEM((4, NB, BLK, BLK), F32),
                pltpu.VMEM((4, 2, Z // 2, SH, BLK, BLK), BF),
                pltpu.VMEM((4, 2, Z // 2, SH, BLK, BLK), BF),
                dma,
                dma((4,)),
                dma((4, 2, Z // 2)),
                dma((4, M)),
                dma((4, M, groups)),
                dma((M, groups, 2)),
                dma((M, groups, 2)),
                dma((4,)),
                dma((4, 2, Z // 2)),
            ],
            compiler_params=pltpu.CompilerParams(
                collective_id=0, has_side_effects=True, vmem_limit_bytes=56 * 1024 * 1024
            ),
        )(section_inputs[0], top_adjoint, right_first[0], left_first[0], right_second[0], left_second[0])
        return adjoint[None], *(grads[f][None] for f in (RF, LF, RS, LS))

    act = P("section", "tok", "hidden")
    weight = P("section", ("hidden", "tok"), None, None)
    return jax.shard_map(
        on_device,
        mesh=mesh,
        in_specs=(act, P("tok", "hidden"), weight, weight, weight, weight),
        out_specs=(act, weight, weight, weight, weight),
        check_vma=False,
    )
```

```python
import functools
import math

import jax
import jax.numpy as jnp
from jax import lax
from jax.experimental import pallas as pl
from jax.experimental.pallas import tpu as pltpu
from jax.sharding import PartitionSpec as P

MESH = pl.DeviceIdType.MESH
BF, F32 = jnp.bfloat16, jnp.float32
BLK = 128
MIC = 64
LANES = 2 * MIC
GRP = 4
COEF = 0.7978845608028654
FM, SM, GM2, GM1 = range(4)
RF, LF, RS, LS = range(4)


def gelu_parts(v):
    squashed = jnp.tanh(COEF * (v + 0.044715 * v * v * v))
    activation = 0.5 * v * (1.0 + squashed)
    derivative = 0.5 * (1.0 + squashed) + 0.5 * v * (1.0 - squashed * squashed) * COEF * (
        1.0 + 3.0 * 0.044715 * v * v
    )
    return activation, derivative


def nn(a, b):
    return lax.dot_general(a, b, (((1,), (0,)), ((), ())), preferred_element_type=F32)


def nt(a, b):
    return lax.dot_general(a, b, (((1,), (1,)), ((), ())), preferred_element_type=F32)


def tn(a, b):
    return lax.dot_general(a, b, (((0,), (0,)), ((), ())), preferred_element_type=F32)


def lanes(b, count=1):
    return pl.ds(pl.multiple_of(b * BLK, BLK), count * BLK)


def kernel(
    S, H, Z, scale,
    x_in, top, rf, lf, rs, ls,
    adj_out, grads,
    x, adj, x_sem, o_sem, ups, send, recv, act, der, gpre, stage, weights, turned, sums, part_send, part_recv,
    top_sem, w_send, w_recv, a_send, a_recv, p_send, p_recv, r_send, r_recv,
):
    sec, h, z = (lax.axis_index(name) for name in ("section", "hidden", "tok"))
    is_last, is_first = sec == S - 1, sec == 0
    early = sec < S - 2
    below, above = lax.rem(sec + S - 1, S), lax.rem(sec + 1, S)
    M = x.shape[0] // MIC
    NB = x.shape[1] // BLK
    SH = NB // Z
    half = NB // 2
    groups = half // GRP

    def rows(m):
        return pl.ds(pl.multiple_of(m * MIC, MIC), MIC)

    def wait(view, sem):
        pltpu.make_async_copy(view, view, sem).wait()

    x_copy = pltpu.make_async_copy(x_in, x, x_sem)
    x_copy.start()
    top_copy = pltpu.make_async_copy(top, ups, top_sem)

    @pl.when(is_last)
    def _():
        top_copy.start()

    barrier = pltpu.get_barrier_semaphore()
    for off in range(1, H):
        pl.semaphore_signal(barrier, 1, device_id={"hidden": lax.rem(h + off, H)}, device_id_type=MESH)
    for off in range(1, Z):
        pl.semaphore_signal(barrier, 1, device_id={"tok": lax.rem(z + off, Z)}, device_id_type=MESH)

    for peer in (below, above):
        pl.semaphore_signal(barrier, 1, device_id={"section": peer}, device_id_type=MESH)

    mine = pl.ds(z * SH, SH)
    for s in range(SH):
        weights[LS, z * SH + s] = ls[s].astype(F32).T.astype(BF)
    weights[RF, mine] = rf[...]
    weights[LF, mine] = lf[...]
    weights[RS, mine] = rs[...]

    for f in range(4):
        sums[f] = jnp.zeros_like(sums[f])

    pl.semaphore_wait(barrier, H - 1 + Z - 1 + 2)

    def hops(f, way):
        return Z // 2 if way == f % 2 else Z - 1 - Z // 2

    def next_on(way):
        return {"tok": lax.rem(z + (1 if way == 0 else Z - 1), Z)}

    def ahead(way, distance):
        return lax.rem(z + (distance if way == 0 else Z - distance), Z)

    def share(index):
        return pl.ds(index * SH, SH)

    def gather_step(f, k):
        for way in (0, 1):
            if k < hops(f, way):
                part = weights.at[f, share(ahead(1 - way, k) if k else z)]
                if k:
                    wait(part, w_recv.at[f, way, k - 1])
                pltpu.make_async_remote_copy(
                    src_ref=part,
                    dst_ref=part,
                    send_sem=w_send.at[f],
                    recv_sem=w_recv.at[f, way, k],
                    device_id=next_on(way),
                    device_id_type=MESH,
                ).start()

    def gather_end(f):
        for way in (0, 1):
            wait(weights.at[f, share(0)], w_recv.at[f, way, hops(f, way) - 1])

    def scatter_step(f, k):
        for way in (0, 1):
            n = hops(f, way)
            if k < n:
                target = ahead(way, n - k)
                if k:
                    wait(part_recv.at[f, way, k - 1], r_recv.at[f, way, k - 1])
                for s in range(SH):
                    total = sums[f, target * SH + s]
                    if k:
                        total = total + part_recv[f, way, k - 1, s].astype(F32)
                    part_send[f, way, k, s] = total.astype(BF)
                pltpu.make_async_remote_copy(
                    src_ref=part_send.at[f, way, k],
                    dst_ref=part_recv.at[f, way, k],
                    send_sem=r_send.at[f],
                    recv_sem=r_recv.at[f, way, k],
                    device_id=next_on(way),
                    device_id_type=MESH,
                ).start()

    def collect(f, turn=False):
        for way in (0, 1):
            last = hops(f, way) - 1
            wait(part_recv.at[f, way, last], r_recv.at[f, way, last])
        for s in range(SH):
            total = sums[f, z * SH + s]
            for way in (0, 1):
                total = total + part_recv[f, way, hops(f, way) - 1, s].astype(F32)
            total = scale * total
            grads[f, s] = total.T if turn else total

    def over_groups(body, before=None, after=None):
        def group(g, carry):
            if before is not None:
                before(g)
            for u in range(GRP):
                body(g * GRP + u)
            if after is not None:
                after(g)
            return carry

        lax.fori_loop(0, groups, group, 0)

    def low(*lead):
        shape = lead + (LANES,)
        return lax.broadcasted_iota(jnp.int32, shape, len(lead)) < MIC

    def put(block, value):
        stage[pl.ds(block, H * half, stride=NB), :] = value.reshape(H * half, LANES)

    def split(value):
        return value.reshape(H, 2, half, LANES)

    def twice(ref, m, b):
        value = ref[rows(m), lanes(b)]
        return jnp.concatenate([value, value], 0)

    def both(f, p):
        return jnp.concatenate([f[p], f[p + half]], 0)

    def diagonal(ref, m, p):
        zero = jnp.zeros((MIC, BLK), BF)
        upper = jnp.concatenate([ref[rows(m), lanes(p)], zero], 1)
        lower = jnp.concatenate([zero, ref[rows(m), lanes(p + half)]], 1)
        return jnp.concatenate([upper, lower], 0)

    def masked(value):
        zero = jnp.zeros_like(value)
        first = low(BLK)
        return jnp.concatenate([jnp.where(first, value, zero), jnp.where(first, zero, value)], 0)

    def put_narrow(weight, ref, m, p):
        for b in (p, p + half):
            out = split(nt(weight[b], twice(ref, m, b)))
            put(b, jnp.where(low(H, half), out[:, 0], out[:, 1]))

    def mine_of(value):
        return jnp.where(low(BLK), value[:BLK], value[BLK:])

    def put_wide(value, p):
        first, second, mask = split(value[:BLK]), split(value[BLK:]), low(H, half)
        other = jnp.where(mask, first[:, 1], second[:, 0]).reshape(H * half, LANES)
        other = pltpu.roll(other, MIC, 1).reshape(H, half, LANES)
        put(p, jnp.where(mask, first[:, 0], other))
        put(p + half, jnp.where(mask, other, second[:, 1]))

    slot = pl.ds(pl.multiple_of(h * NB, NB), NB)

    def staged(d, g):
        at = pl.multiple_of((d * half + g * GRP) * NB, NB)
        return stage[pl.ds(at, GRP * NB), :].astype(BF).reshape(GRP, NB, LANES)

    def exchange(p, m):
        def quarter(g, carry):
            part = pl.ds(g * GRP, GRP)
            for off in sorted(range(1, H), key=lambda o: abs(o - H // 2)):
                peer = lax.rem(h + off, H)
                send[p, m, peer, part] = staged(peer, g)
                pltpu.make_async_remote_copy(
                    src_ref=send.at[p, m, peer, part],
                    dst_ref=recv.at[p, m, part, slot, :],
                    send_sem=a_send.at[p, m],
                    recv_sem=a_recv.at[p, m, g],
                    device_id={"hidden": peer},
                    device_id_type=MESH,
                ).start()
            recv[p, m, part, slot, :] = staged(h, g)
            return carry

        lax.fori_loop(0, groups, quarter, 0)

    def arrival(p, m):
        def before(g):
            wait(recv.at[p, m, pl.ds(g * GRP, GRP), pl.ds(0, BLK - NB)], a_recv.at[p, m, g])

        return before

    def first_mid(m):
        over_groups(lambda p: put_narrow(weights.at[RF], x, m, p))
        exchange(FM, m)

    def activations(m):
        def body(p):
            a, d = gelu_parts(mine_of(nn(both(weights.at[LF], p), recv[FM, m, p])))
            act[m, p] = a.astype(BF)
            der[m, p] = d

        over_groups(body, before=arrival(FM, m))

    def second_mid(m):
        over_groups(lambda p: put_wide(nn(both(weights.at[RS], p), act[m, p]), p))
        exchange(SM, m)

    def passed(m, g, q):
        return rows(m), lanes(q * half + g * GRP, GRP)

    def grad_mid_second(m, arrives):
        def before(g):
            for q in (0, 1):
                wait(ups.at[passed(m, g, q)], p_recv.at[m, g, q])

        over_groups(
            lambda p: put_narrow(weights.at[LS], ups, m, p),
            before=before if arrives else None,
        )
        exchange(GM2, m)

    def grad_mid_first(m):
        def body(p):
            grad = mine_of(nn(both(turned.at[1], p), recv[GM2, m, p]))
            pre = (grad * der[m, p]).astype(BF)
            gpre[m, p] = pre
            put_wide(nn(both(turned.at[0], p), pre), p)

        over_groups(body, before=arrival(GM2, m))
        exchange(GM1, m)

    def input_adjoint(m):
        def body(p):
            weight = jnp.concatenate([weights[RF, p], weights[RF, p + half]], 1)
            grad = tn(recv[GM1, m, p], weight)
            for q in (0, 1):
                at = lanes(p + q * half)
                part = grad[q * MIC : (q + 1) * MIC, q * BLK : (q + 1) * BLK]
                adj[rows(m), at] = (ups[rows(m), at].astype(F32) + part).astype(BF)

        def after(g):
            @pl.when(jnp.logical_not(is_first))
            def _():
                for q in (0, 1):
                    part = passed(m, g, q)
                    pltpu.make_async_remote_copy(
                        src_ref=adj.at[part],
                        dst_ref=ups.at[part],
                        send_sem=p_send.at[m, g, q],
                        recv_sem=p_recv.at[m, g, q],
                        device_id={"section": below},
                        device_id_type=MESH,
                    ).start()

        over_groups(body, before=arrival(GM1, m), after=after)
        pltpu.make_async_copy(adj.at[rows(m)], adj_out.at[rows(m)], o_sem.at[m]).start()

    def wide_gradients(m):
        def body(p):
            for f, left, right in (
                (RS, recv[GM2, m, p], act[m, p]),
                (LF, gpre[m, p], recv[FM, m, p]),
            ):
                grad = nt(masked(left), right)
                sums[f, p] += grad[:BLK]
                sums[f, p + half] += grad[BLK:]

        over_groups(body)

    def narrow_gradient(f, m, p, left, ref):
        grad = nn(left, diagonal(ref, m, p))
        sums[f, p] += grad[:, :BLK]
        sums[f, p + half] += grad[:, BLK:]

    def gradient_rf(m):
        over_groups(lambda p: narrow_gradient(RF, m, p, recv[GM1, m, p], x))

    def gradient_ls(m):
        over_groups(
            lambda p: narrow_gradient(LS, m, p, recv[SM, m, p], ups), before=arrival(SM, m)
        )

    def turn(p):
        for b in (p, p + half):
            turned[0, b] = weights[LF, b].astype(F32).T.astype(BF)
            turned[1, b] = weights[RS, b].astype(F32).T.astype(BF)

    steps = Z // 2

    def advance(*items):
        for f, k in items:
            if k < steps:
                gather_step(f, k)
            else:
                gather_end(f)

    for k in range(steps):
        advance((RF, k), (LS, k))
    advance((LF, 0), (RS, 0), (RF, steps), (LS, steps))

    def repeat(first, end, body):
        def step(m, carry):
            body(m)
            return carry

        lax.fori_loop(first, end, step, 0)

    def chain_of_last():
        def feed(m):
            first_mid(m)
            grad_mid_second(m, False)

        top_copy.wait()
        feed(0)
        advance((LF, 1), (RS, 1))
        feed(1)
        advance((LF, 2), (RS, 2), (LF, 3), (RS, 3), (LF, 4), (RS, 4))
        over_groups(turn)
        activations(0)

        def steady(m):
            grad_mid_first(m)
            feed(m + 2)
            activations(m + 1)
            input_adjoint(m)

        repeat(0, M - 2, steady)
        grad_mid_first(M - 2)
        activations(M - 1)
        input_adjoint(M - 2)
        grad_mid_first(M - 1)
        input_adjoint(M - 1)
        repeat(0, M, second_mid)

        def own_gradients(m):
            wide_gradients(m)
            gradient_rf(m)

        repeat(0, M, own_gradients)
        repeat(0, M, gradient_ls)
        for f, k in ((LS, 0), (RS, 0), (LF, 0), (LS, 1), (LS, 2), (LS, 3)):
            scatter_step(f, k)

    def chain_of_others():
        for k in range(1, steps):
            first_mid(k - 1)
            advance((LF, k), (RS, k))
        repeat(steps - 1, M, first_mid)
        advance((LF, steps), (RS, steps))

        def forward(m):
            activations(m)
            pl.when(early)(lambda: second_mid(m))

        repeat(0, M, forward)
        over_groups(turn)

        def steady(m):
            grad_mid_first(m)
            wide_gradients(m)
            grad_mid_second(m + 1, True)
            pl.when(early)(lambda: gradient_ls(m + 1))
            input_adjoint(m)
            gradient_rf(m)

        grad_mid_second(0, True)
        pl.when(early)(lambda: gradient_ls(0))
        repeat(0, M - 2, steady)
        m = M - 2
        grad_mid_first(m)
        grad_mid_second(m + 1, True)
        pl.when(early)(lambda: gradient_ls(M - 1))
        pl.when(early)(lambda: scatter_step(LS, 0))
        wide_gradients(m)
        input_adjoint(m)
        pl.when(early)(lambda: scatter_step(LS, 1))
        gradient_rf(m)
        m = M - 1
        grad_mid_first(m)
        pl.when(early)(lambda: scatter_step(LS, 2))
        wide_gradients(m)
        scatter_step(RS, 0)
        scatter_step(LF, 0)
        pl.when(early)(lambda: scatter_step(LS, 3))
        input_adjoint(m)
        gradient_rf(m)

        @pl.when(jnp.logical_not(early))
        def _():
            repeat(0, M, second_mid)
            repeat(0, M, gradient_ls)
            for k in range(steps):
                scatter_step(LS, k)

    x_copy.wait()
    pl.when(is_last)(chain_of_last)
    pl.when(jnp.logical_not(is_last))(chain_of_others)

    scatter_step(RF, 0)
    for k in range(1, steps):
        for f in (RS, LF, RF):
            scatter_step(f, k)
    collect(LS, True)
    collect(RS)
    collect(LF)
    collect(RF)

    for m in range(M):
        pltpu.make_async_copy(adj.at[rows(m)], adj_out.at[rows(m)], o_sem.at[m]).wait()
    for f in range(4):
        wait(weights.at[f, pl.ds(0, (Z - 1) * SH)], w_send.at[f])
        wait(weights.at[f, pl.ds(0, (Z - 1) * SH)], r_send.at[f])
    for p in range(4):
        for m in range(M):
            wait(send.at[p, m, pl.ds(0, H - 1)], a_send.at[p, m])

    @pl.when(jnp.logical_not(is_first))
    def _():
        for m in range(M):
            for g in range(groups):
                for q in (0, 1):
                    wait(adj.at[passed(m, g, q)], p_send.at[m, g, q])


def solution(mesh):
    S, H, Z = (mesh.shape[name] for name in ("section", "hidden", "tok"))

    def on_device(section_inputs, top_adjoint, right_first, left_first, right_second, left_second):
        tokens, width = top_adjoint.shape
        M, NB, SH = tokens // MIC, width // BLK, right_first.shape[1]
        half = NB // 2
        groups = half // GRP
        scale = 1.0 / math.sqrt(tokens * Z)
        vmem = pl.BlockSpec(memory_space=pltpu.VMEM)
        dma = pltpu.SemaphoreType.DMA
        adjoint, grads = pl.pallas_call(
            functools.partial(kernel, S, H, Z, scale),
            out_shape=[
                jax.ShapeDtypeStruct((tokens, width), BF),
                jax.ShapeDtypeStruct((4, SH, BLK, BLK), F32),
            ],
            in_specs=[pl.BlockSpec(memory_space=pl.ANY)] * 2 + [vmem] * 4,
            out_specs=[pl.BlockSpec(memory_space=pl.ANY), vmem],
            scratch_shapes=[
                pltpu.VMEM((tokens, width), BF),
                pltpu.VMEM((tokens, width), BF),
                dma,
                dma((M,)),
                pltpu.VMEM((tokens, width), BF),
                pltpu.VMEM((4, M, H, half, NB, LANES), BF),
                pltpu.VMEM((4, M, half, BLK, LANES), BF),
                pltpu.VMEM((M, half, BLK, LANES), BF),
                pltpu.VMEM((M, half, BLK, LANES), F32),
                pltpu.VMEM((M, half, BLK, LANES), BF),
                pltpu.VMEM((H * half * NB, LANES), F32),
                pltpu.VMEM((4, NB, BLK, BLK), BF),
                pltpu.VMEM((2, NB, BLK, BLK), BF),
                pltpu.VMEM((4, NB, BLK, BLK), F32),
                pltpu.VMEM((4, 2, Z // 2, SH, BLK, BLK), BF),
                pltpu.VMEM((4, 2, Z // 2, SH, BLK, BLK), BF),
                dma,
                dma((4,)),
                dma((4, 2, Z // 2)),
                dma((4, M)),
                dma((4, M, groups)),
                dma((M, groups, 2)),
                dma((M, groups, 2)),
                dma((4,)),
                dma((4, 2, Z // 2)),
            ],
            compiler_params=pltpu.CompilerParams(
                collective_id=0, has_side_effects=True, vmem_limit_bytes=56 * 1024 * 1024
            ),
        )(section_inputs[0], top_adjoint, right_first[0], left_first[0], right_second[0], left_second[0])
        return adjoint[None], *(grads[f][None] for f in (RF, LF, RS, LS))

    act = P("section", "tok", "hidden")
    weight = P("section", ("hidden", "tok"), None, None)
    return jax.shard_map(
        on_device,
        mesh=mesh,
        in_specs=(act, P("tok", "hidden"), weight, weight, weight, weight),
        out_specs=(act, weight, weight, weight, weight),
        check_vma=False,
    )
```

```python
import functools
import math

import jax
import jax.numpy as jnp
from jax import lax
from jax.experimental import pallas as pl
from jax.experimental.pallas import tpu as pltpu
from jax.sharding import PartitionSpec as P

MESH = pl.DeviceIdType.MESH
BF, F32 = jnp.bfloat16, jnp.float32
BLK = 128
MIC = 64
LANES = 2 * MIC
GRP = 4
COEF = 0.7978845608028654
FM, SM, GM2, GM1 = range(4)
RF, LF, RS, LS = range(4)


def gelu_parts(v):
    squashed = jnp.tanh(COEF * (v + 0.044715 * v * v * v))
    activation = 0.5 * v * (1.0 + squashed)
    derivative = 0.5 * (1.0 + squashed) + 0.5 * v * (1.0 - squashed * squashed) * COEF * (
        1.0 + 3.0 * 0.044715 * v * v
    )
    return activation, derivative


def nn(a, b):
    return lax.dot_general(a, b, (((1,), (0,)), ((), ())), preferred_element_type=F32)


def nt(a, b):
    return lax.dot_general(a, b, (((1,), (1,)), ((), ())), preferred_element_type=F32)


def tn(a, b):
    return lax.dot_general(a, b, (((0,), (0,)), ((), ())), preferred_element_type=F32)


def lanes(b, count=1):
    return pl.ds(pl.multiple_of(b * BLK, BLK), count * BLK)


def kernel(
    S, H, Z, scale,
    x_in, top, rf, lf, rs, ls,
    adj_out, grads,
    x, adj, x_sem, o_sem, ups, send, recv, act, der, gpre, stage, weights, turned, sums, part_send, part_recv,
    top_sem, w_send, w_recv, a_send, a_recv, p_send, p_recv, r_send, r_recv,
):
    sec, h, z = (lax.axis_index(name) for name in ("section", "hidden", "tok"))
    is_last, is_first = sec == S - 1, sec == 0
    early = sec < S - 2
    below, above = lax.rem(sec + S - 1, S), lax.rem(sec + 1, S)
    M = x.shape[0] // MIC
    NB = x.shape[1] // BLK
    SH = NB // Z
    half = NB // 2
    groups = half // GRP

    def rows(m):
        return pl.ds(pl.multiple_of(m * MIC, MIC), MIC)

    def wait(view, sem):
        pltpu.make_async_copy(view, view, sem).wait()

    x_copy = pltpu.make_async_copy(x_in, x, x_sem)
    x_copy.start()
    top_copy = pltpu.make_async_copy(top, ups, top_sem)

    @pl.when(is_last)
    def _():
        top_copy.start()

    barrier = pltpu.get_barrier_semaphore()
    for off in range(1, H):
        pl.semaphore_signal(barrier, 1, device_id={"hidden": lax.rem(h + off, H)}, device_id_type=MESH)
    for off in range(1, Z):
        pl.semaphore_signal(barrier, 1, device_id={"tok": lax.rem(z + off, Z)}, device_id_type=MESH)

    for peer in (below, above):
        pl.semaphore_signal(barrier, 1, device_id={"section": peer}, device_id_type=MESH)

    mine = pl.ds(z * SH, SH)
    for s in range(SH):
        weights[LS, z * SH + s] = ls[s].astype(F32).T.astype(BF)
    weights[RF, mine] = rf[...]
    weights[LF, mine] = lf[...]
    weights[RS, mine] = rs[...]

    for f in range(4):
        sums[f] = jnp.zeros_like(sums[f])

    pl.semaphore_wait(barrier, H - 1 + Z - 1 + 2)

    def hops(f, way):
        return Z // 2 if way == f % 2 else Z - 1 - Z // 2

    def next_on(way):
        return {"tok": lax.rem(z + (1 if way == 0 else Z - 1), Z)}

    def ahead(way, distance):
        return lax.rem(z + (distance if way == 0 else Z - distance), Z)

    def share(index):
        return pl.ds(index * SH, SH)

    def gather_step(f, k):
        for way in (0, 1):
            if k < hops(f, way):
                origin = ahead(1 - way, k) if k else z
                for s in range(SH):
                    part = weights.at[f, origin * SH + s]
                    if k:
                        wait(part, w_recv.at[f, way, k - 1, s])
                    pltpu.make_async_remote_copy(
                        src_ref=part,
                        dst_ref=part,
                        send_sem=w_send.at[f],
                        recv_sem=w_recv.at[f, way, k, s],
                        device_id=next_on(way),
                        device_id_type=MESH,
                    ).start()

    def gather_end(f):
        for way in (0, 1):
            for s in range(SH):
                wait(weights.at[f, s], w_recv.at[f, way, hops(f, way) - 1, s])

    def scatter_step(f, k):
        for way in (0, 1):
            n = hops(f, way)
            if k < n:
                target = ahead(way, n - k)
                for s in range(SH):
                    total = sums[f, target * SH + s]
                    if k:
                        wait(part_recv.at[f, way, k - 1, s], r_recv.at[f, way, k - 1, s])
                        total = total + part_recv[f, way, k - 1, s].astype(F32)
                    part_send[f, way, k, s] = total.astype(BF)
                    pltpu.make_async_remote_copy(
                        src_ref=part_send.at[f, way, k, s],
                        dst_ref=part_recv.at[f, way, k, s],
                        send_sem=r_send.at[f],
                        recv_sem=r_recv.at[f, way, k, s],
                        device_id=next_on(way),
                        device_id_type=MESH,
                    ).start()

    def collect(f, turn=False):
        for way in (0, 1):
            last = hops(f, way) - 1
            for s in range(SH):
                wait(part_recv.at[f, way, last, s], r_recv.at[f, way, last, s])
        for s in range(SH):
            total = sums[f, z * SH + s]
            for way in (0, 1):
                total = total + part_recv[f, way, hops(f, way) - 1, s].astype(F32)
            total = scale * total
            grads[f, s] = total.T if turn else total

    def over_groups(body, before=None, after=None):
        def group(g, carry):
            if before is not None:
                before(g)
            for u in range(GRP):
                body(g * GRP + u)
            if after is not None:
                after(g)
            return carry

        lax.fori_loop(0, groups, group, 0)

    def low(*lead):
        shape = lead + (LANES,)
        return lax.broadcasted_iota(jnp.int32, shape, len(lead)) < MIC

    def put(block, value):
        stage[pl.ds(block, H * half, stride=NB), :] = value.reshape(H * half, LANES)

    def split(value):
        return value.reshape(H, 2, half, LANES)

    def twice(ref, m, b):
        value = ref[rows(m), lanes(b)]
        return jnp.concatenate([value, value], 0)

    def both(f, p):
        return jnp.concatenate([f[p], f[p + half]], 0)

    def diagonal(ref, m, p):
        zero = jnp.zeros((MIC, BLK), BF)
        upper = jnp.concatenate([ref[rows(m), lanes(p)], zero], 1)
        lower = jnp.concatenate([zero, ref[rows(m), lanes(p + half)]], 1)
        return jnp.concatenate([upper, lower], 0)

    def masked(value):
        zero = jnp.zeros_like(value)
        first = low(BLK)
        return jnp.concatenate([jnp.where(first, value, zero), jnp.where(first, zero, value)], 0)

    def put_narrow(weight, ref, m, p):
        for b in (p, p + half):
            out = split(nt(weight[b], twice(ref, m, b)))
            put(b, jnp.where(low(H, half), out[:, 0], out[:, 1]))

    def mine_of(value):
        return jnp.where(low(BLK), value[:BLK], value[BLK:])

    def put_wide(value, p):
        first, second, mask = split(value[:BLK]), split(value[BLK:]), low(H, half)
        other = jnp.where(mask, first[:, 1], second[:, 0]).reshape(H * half, LANES)
        other = pltpu.roll(other, MIC, 1).reshape(H, half, LANES)
        put(p, jnp.where(mask, first[:, 0], other))
        put(p + half, jnp.where(mask, other, second[:, 1]))

    slot = pl.ds(pl.multiple_of(h * NB, NB), NB)

    def staged(d, g):
        at = pl.multiple_of((d * half + g * GRP) * NB, NB)
        return stage[pl.ds(at, GRP * NB), :].astype(BF).reshape(GRP, NB, LANES)

    def exchange(p, m):
        def quarter(g, carry):
            part = pl.ds(g * GRP, GRP)
            for off in sorted(range(1, H), key=lambda o: abs(o - H // 2)):
                peer = lax.rem(h + off, H)
                send[p, m, peer, part] = staged(peer, g)
                pltpu.make_async_remote_copy(
                    src_ref=send.at[p, m, peer, part],
                    dst_ref=recv.at[p, m, part, slot, :],
                    send_sem=a_send.at[p, m],
                    recv_sem=a_recv.at[p, m, g],
                    device_id={"hidden": peer},
                    device_id_type=MESH,
                ).start()
            recv[p, m, part, slot, :] = staged(h, g)
            return carry

        lax.fori_loop(0, groups, quarter, 0)

    def arrival(p, m):
        def before(g):
            wait(recv.at[p, m, pl.ds(g * GRP, GRP), pl.ds(0, BLK - NB)], a_recv.at[p, m, g])

        return before

    def first_mid(m):
        over_groups(lambda p: put_narrow(weights.at[RF], x, m, p))
        exchange(FM, m)

    def activations(m):
        def body(p):
            a, d = gelu_parts(mine_of(nn(both(weights.at[LF], p), recv[FM, m, p])))
            act[m, p] = a.astype(BF)
            der[m, p] = d

        over_groups(body, before=arrival(FM, m))

    def second_mid(m):
        over_groups(lambda p: put_wide(nn(both(weights.at[RS], p), act[m, p]), p))
        exchange(SM, m)

    def passed(m, g, q):
        return rows(m), lanes(q * half + g * GRP, GRP)

    def grad_mid_second(m, arrives):
        def before(g):
            for q in (0, 1):
                wait(ups.at[passed(m, g, q)], p_recv.at[m, g, q])

        over_groups(
            lambda p: put_narrow(weights.at[LS], ups, m, p),
            before=before if arrives else None,
        )
        exchange(GM2, m)

    def grad_mid_first(m):
        def body(p):
            grad = mine_of(nn(both(turned.at[1], p), recv[GM2, m, p]))
            pre = (grad * der[m, p]).astype(BF)
            gpre[m, p] = pre
            put_wide(nn(both(turned.at[0], p), pre), p)

        over_groups(body, before=arrival(GM2, m))
        exchange(GM1, m)

    def input_adjoint(m):
        def body(p):
            weight = jnp.concatenate([weights[RF, p], weights[RF, p + half]], 1)
            grad = tn(recv[GM1, m, p], weight)
            for q in (0, 1):
                at = lanes(p + q * half)
                part = grad[q * MIC : (q + 1) * MIC, q * BLK : (q + 1) * BLK]
                adj[rows(m), at] = (ups[rows(m), at].astype(F32) + part).astype(BF)

        def after(g):
            @pl.when(jnp.logical_not(is_first))
            def _():
                for q in (0, 1):
                    part = passed(m, g, q)
                    pltpu.make_async_remote_copy(
                        src_ref=adj.at[part],
                        dst_ref=ups.at[part],
                        send_sem=p_send.at[m, g, q],
                        recv_sem=p_recv.at[m, g, q],
                        device_id={"section": below},
                        device_id_type=MESH,
                    ).start()

        over_groups(body, before=arrival(GM1, m), after=after)
        pltpu.make_async_copy(adj.at[rows(m)], adj_out.at[rows(m)], o_sem.at[m]).start()

    def wide_gradients(m):
        def body(p):
            for f, left, right in (
                (RS, recv[GM2, m, p], act[m, p]),
                (LF, gpre[m, p], recv[FM, m, p]),
            ):
                grad = nt(masked(left), right)
                sums[f, p] += grad[:BLK]
                sums[f, p + half] += grad[BLK:]

        over_groups(body)

    def narrow_gradient(f, m, p, left, ref):
        grad = nn(left, diagonal(ref, m, p))
        sums[f, p] += grad[:, :BLK]
        sums[f, p + half] += grad[:, BLK:]

    def gradient_rf(m):
        over_groups(lambda p: narrow_gradient(RF, m, p, recv[GM1, m, p], x))

    def gradient_ls(m):
        over_groups(
            lambda p: narrow_gradient(LS, m, p, recv[SM, m, p], ups), before=arrival(SM, m)
        )

    def turn(p):
        for b in (p, p + half):
            turned[0, b] = weights[LF, b].astype(F32).T.astype(BF)
            turned[1, b] = weights[RS, b].astype(F32).T.astype(BF)

    steps = Z // 2

    def advance(*items):
        for f, k in items:
            if k < steps:
                gather_step(f, k)
            else:
                gather_end(f)

    for k in range(steps):
        advance((RF, k), (LS, k))
    advance((LF, 0), (RS, 0), (RF, steps), (LS, steps))

    def repeat(first, end, body):
        def step(m, carry):
            body(m)
            return carry

        lax.fori_loop(first, end, step, 0)

    def chain_of_last():
        def feed(m):
            first_mid(m)
            grad_mid_second(m, False)

        top_copy.wait()
        feed(0)
        advance((LF, 1), (RS, 1))
        feed(1)
        advance((LF, 2), (RS, 2), (LF, 3), (RS, 3), (LF, 4), (RS, 4))
        over_groups(turn)
        activations(0)

        def steady(m):
            grad_mid_first(m)
            feed(m + 2)
            activations(m + 1)
            input_adjoint(m)

        repeat(0, M - 2, steady)
        grad_mid_first(M - 2)
        activations(M - 1)
        input_adjoint(M - 2)
        grad_mid_first(M - 1)
        input_adjoint(M - 1)
        repeat(0, M, second_mid)

        def own_gradients(m):
            wide_gradients(m)
            gradient_rf(m)

        repeat(0, M, own_gradients)
        repeat(0, M, gradient_ls)
        for f, k in ((LS, 0), (RS, 0), (LF, 0), (LS, 1), (LS, 2), (LS, 3)):
            scatter_step(f, k)

    def chain_of_others():
        for k in range(1, steps):
            first_mid(k - 1)
            advance((LF, k), (RS, k))
        repeat(steps - 1, M, first_mid)
        advance((LF, steps), (RS, steps))

        def forward(m):
            activations(m)
            pl.when(early)(lambda: second_mid(m))

        repeat(0, M, forward)
        over_groups(turn)

        def steady(m):
            grad_mid_first(m)
            wide_gradients(m)
            grad_mid_second(m + 1, True)
            pl.when(early)(lambda: gradient_ls(m + 1))
            input_adjoint(m)
            gradient_rf(m)

        grad_mid_second(0, True)
        pl.when(early)(lambda: gradient_ls(0))
        repeat(0, M - 2, steady)
        m = M - 2
        grad_mid_first(m)
        grad_mid_second(m + 1, True)
        pl.when(early)(lambda: gradient_ls(M - 1))
        pl.when(early)(lambda: scatter_step(LS, 0))
        wide_gradients(m)
        input_adjoint(m)
        pl.when(early)(lambda: scatter_step(LS, 1))
        gradient_rf(m)
        m = M - 1
        grad_mid_first(m)
        pl.when(early)(lambda: scatter_step(LS, 2))
        wide_gradients(m)
        scatter_step(RS, 0)
        scatter_step(LF, 0)
        pl.when(early)(lambda: scatter_step(LS, 3))
        input_adjoint(m)
        gradient_rf(m)

        @pl.when(jnp.logical_not(early))
        def _():
            repeat(0, M, second_mid)
            repeat(0, M, gradient_ls)
            for k in range(steps):
                scatter_step(LS, k)

    x_copy.wait()
    pl.when(is_last)(chain_of_last)
    pl.when(jnp.logical_not(is_last))(chain_of_others)

    scatter_step(RF, 0)
    for k in range(1, steps):
        for f in (RS, LF, RF):
            scatter_step(f, k)
    collect(LS, True)
    collect(RS)
    collect(LF)
    collect(RF)

    for m in range(M):
        pltpu.make_async_copy(adj.at[rows(m)], adj_out.at[rows(m)], o_sem.at[m]).wait()
    for f in range(4):
        wait(weights.at[f, pl.ds(0, (Z - 1) * SH)], w_send.at[f])
        wait(weights.at[f, pl.ds(0, (Z - 1) * SH)], r_send.at[f])
    for p in range(4):
        for m in range(M):
            wait(send.at[p, m, pl.ds(0, H - 1)], a_send.at[p, m])

    @pl.when(jnp.logical_not(is_first))
    def _():
        for m in range(M):
            for g in range(groups):
                for q in (0, 1):
                    wait(adj.at[passed(m, g, q)], p_send.at[m, g, q])


def solution(mesh):
    S, H, Z = (mesh.shape[name] for name in ("section", "hidden", "tok"))

    def on_device(section_inputs, top_adjoint, right_first, left_first, right_second, left_second):
        tokens, width = top_adjoint.shape
        M, NB, SH = tokens // MIC, width // BLK, right_first.shape[1]
        half = NB // 2
        groups = half // GRP
        scale = 1.0 / math.sqrt(tokens * Z)
        vmem = pl.BlockSpec(memory_space=pltpu.VMEM)
        dma = pltpu.SemaphoreType.DMA
        adjoint, grads = pl.pallas_call(
            functools.partial(kernel, S, H, Z, scale),
            out_shape=[
                jax.ShapeDtypeStruct((tokens, width), BF),
                jax.ShapeDtypeStruct((4, SH, BLK, BLK), F32),
            ],
            in_specs=[pl.BlockSpec(memory_space=pl.ANY)] * 2 + [vmem] * 4,
            out_specs=[pl.BlockSpec(memory_space=pl.ANY), vmem],
            scratch_shapes=[
                pltpu.VMEM((tokens, width), BF),
                pltpu.VMEM((tokens, width), BF),
                dma,
                dma((M,)),
                pltpu.VMEM((tokens, width), BF),
                pltpu.VMEM((4, M, H, half, NB, LANES), BF),
                pltpu.VMEM((4, M, half, BLK, LANES), BF),
                pltpu.VMEM((M, half, BLK, LANES), BF),
                pltpu.VMEM((M, half, BLK, LANES), F32),
                pltpu.VMEM((M, half, BLK, LANES), BF),
                pltpu.VMEM((H * half * NB, LANES), F32),
                pltpu.VMEM((4, NB, BLK, BLK), BF),
                pltpu.VMEM((2, NB, BLK, BLK), BF),
                pltpu.VMEM((4, NB, BLK, BLK), F32),
                pltpu.VMEM((4, 2, Z // 2, SH, BLK, BLK), BF),
                pltpu.VMEM((4, 2, Z // 2, SH, BLK, BLK), BF),
                dma,
                dma((4,)),
                dma((4, 2, Z // 2, SH)),
                dma((4, M)),
                dma((4, M, groups)),
                dma((M, groups, 2)),
                dma((M, groups, 2)),
                dma((4,)),
                dma((4, 2, Z // 2, SH)),
            ],
            compiler_params=pltpu.CompilerParams(
                collective_id=0, has_side_effects=True, vmem_limit_bytes=56 * 1024 * 1024
            ),
        )(section_inputs[0], top_adjoint, right_first[0], left_first[0], right_second[0], left_second[0])
        return adjoint[None], *(grads[f][None] for f in (RF, LF, RS, LS))

    act = P("section", "tok", "hidden")
    weight = P("section", ("hidden", "tok"), None, None)
    return jax.shard_map(
        on_device,
        mesh=mesh,
        in_specs=(act, P("tok", "hidden"), weight, weight, weight, weight),
        out_specs=(act, weight, weight, weight, weight),
        check_vma=False,
    )
```
